32 devices in a mesh: section: 4 (over y, core), dp: 8 (over z, x).
Axes of the slice: x: 2, y: 2, z: 4, core: 2. Of those that a mesh axis runs over, the one named last changes fastest.
Arguments:
- queries: bfloat16 [4, 1024, 8192], P('section', 'dp'), may hold values from -48 to 48
- image_kv: bfloat16 [4, 2, 32, 1024], P(None, None, ('section', 'dp')), may hold values from -4 to 4
- visible: int32 [1024], P('dp'), may hold values from 0 to 32, as said below
- gate: float32 [4], P('section'), may hold values from 0.3 to 2
Outputs:
- cross_out: bfloat16 [4, 1024, 8192], P('section', 'dp')
The draws below stay inside these ranges and needn't reach their ends.
Inputs may be any that keep to these rules, and one draw needn't show every extreme that they name: `visible`: every value is a multiple of 8; the last token of each aligned block of 128 text tokens sees all 32 image tokens.
All inputs are finite; a program needn't handle non-finite values.
Results may differ from the reference program's by a relative error of at most 0.0065.
Values may be sent and summed in bfloat16 or wider, within the bound.
A program may use at most 64 MiB of HBM per device.

```python
import jax
import jax.numpy as jnp
from jax import lax

H = 64
KVH = 8
HD = 128
TILES = 4
TXT_DEV = 128
TXT = 1024
IMG = 32
IMG_TILE = 8
N_SECTION = 4


def float_pair(key):
    base = jax.random.fold_in(key, 11)
    key_query = jax.random.fold_in(base, 1)
    key_image = jax.random.fold_in(base, 2)
    image = jnp.clip(jax.random.normal(key_image, (N_SECTION, 2, IMG, KVH * HD), jnp.float32), -4.0, 4.0)
    query = jnp.clip(jax.random.normal(key_query, (N_SECTION, TXT, H * HD), jnp.float32), -4.0, 4.0)
    return (query, image)


def draw_queries(key, part):
    return float_pair(key)[0].astype(jnp.bfloat16)


def draw_image_kv(key, part):
    return float_pair(key)[1].astype(jnp.bfloat16)


def draw_visible(key, part):
    tiles_seen = jax.random.randint(jax.random.fold_in(key, 23), (TXT,), 0, TILES + 1)
    last_row = jnp.arange(TXT, dtype=jnp.int32) % TXT_DEV == TXT_DEV - 1
    tiles_seen = jnp.where(last_row, TILES, tiles_seen)
    return (tiles_seen * IMG_TILE).astype(jnp.int32)


def shard_levels(own_key, dims, cuts, low, top_value):
    level = 1.0
    for dim, shards_of in cuts:
        heights = jax.random.uniform(jax.random.fold_in(jax.random.fold_in(own_key, 6), dim), (shards_of,), jnp.float32, low / len(cuts), top_value / len(cuts))
        level = level * jnp.repeat(jnp.exp(heights), dims[dim] // shards_of).reshape((-1,) + (1,) * (len(dims) - 1 - dim))
    return level


def setup_inputs(seed: int = 0) -> dict:
    key_of = jax.random.split(jax.random.key(seed), 5)
    queries = draw_queries(jax.random.fold_in(key_of[4], 71), 0)
    image_kv = draw_image_kv(jax.random.fold_in(key_of[4], 71), 0)
    visible = draw_visible(jax.random.fold_in(key_of[4], 71), 0)
    gate = jnp.clip(0.3 + 1.7 * jax.random.uniform(key_of[3], (N_SECTION,), jnp.float32) ** shard_levels(key_of[3], (N_SECTION,), ((0, 4),), -0.2, 0.2), 0.3, 2.0)
    return dict(queries=queries, image_kv=image_kv, visible=visible, gate=gate)


def layer_attention(query_rows, keys, vals, seen, gate_value):
    rows = query_rows.shape[0]
    query = query_rows.astype(jnp.float32).reshape(rows, KVH, H // KVH, HD)
    scores = jnp.einsum('tkgd,nkd->kgtn', query, keys) / jnp.sqrt(jnp.float32(HD))
    positions = jnp.arange(IMG, dtype=jnp.int32)
    live = positions[None, :] < seen[:, None]
    capped = jnp.where(live, scores, -1e+30)
    top = lax.optimization_barrier(jnp.max(capped, axis=-1))
    expo = jnp.where(live, jnp.exp(capped - top[..., None]), 0.0)
    denom = lax.optimization_barrier(jnp.sum(expo, axis=-1))
    weights = expo.astype(jnp.bfloat16).astype(jnp.float32)
    acc = jnp.einsum('kgtn,nkd->kgtd', weights, vals)
    result = acc / jnp.where(denom > 0, denom, 1.0)[..., None]
    result = jnp.transpose(result, (2, 0, 1, 3)).reshape(rows, H * HD)
    result = jnp.where((seen > 0)[:, None], result, 0.0) * jnp.tanh(gate_value)
    return result.astype(jnp.bfloat16)

def reference(queries, image_kv, visible, gate):
    outputs = []
    blocks = TXT // TXT_DEV
    for layer in range(N_SECTION):
        keys = image_kv[layer, 0].astype(jnp.float32).reshape(IMG, KVH, HD)
        vals = image_kv[layer, 1].astype(jnp.float32).reshape(IMG, KVH, HD)
        query_blocks = queries[layer].reshape(blocks, TXT_DEV, H * HD)
        seen_blocks = visible.reshape(blocks, TXT_DEV)

        def run(pair):
            return layer_attention(pair[0], keys, vals, pair[1], gate[layer])
        outputs.append(lax.map(run, (query_blocks, seen_blocks)).reshape(TXT, H * HD))
    return jnp.stack(outputs, axis=0)
```

```python
import functools
import math

import jax
import jax.numpy as jnp
from jax import lax
from jax.experimental import pallas as pl
from jax.experimental.pallas import tpu as pltpu
from jax.sharding import PartitionSpec as P

HD = 128
LOG2E = math.log2(math.e)


def gather_kernel(sections, dps, kv_ref, out_ref, stage, send, slots, wide, send_sem, recv_sem):
    count = sections * dps
    my_section = lax.axis_index("section")
    my_dp = lax.axis_index("dp")
    me = my_section * dps + my_dp
    img_dev = kv_ref.shape[1]
    heads = kv_ref.shape[3] // HD
    per_token = 2 * heads
    tokens = count * img_dev

    barrier = pltpu.get_barrier_semaphore()

    def peer_of(step):
        peer = lax.rem(me + step, count)
        return lax.div(peer, dps), lax.rem(peer, dps)

    def greet(step, unused):
        section, dp = peer_of(step)
        pl.semaphore_signal(barrier, inc=1, device_id={"section": section, "dp": dp})
        return unused

    lax.fori_loop(1, count, greet, 0)

    for layer in range(sections):
        for token in range(img_dev):
            rows = kv_ref[layer, token].astype(jnp.float32)
            for part in range(2):
                for head in range(heads):
                    at = token * per_token + part * heads + head
                    stage[layer, at : at + 1, :] = rows[part : part + 1, head * HD : (head + 1) * HD]
        send[layer] = stage[layer].astype(send.dtype)

    pl.semaphore_wait(barrier, count - 1)

    def post(step, unused):
        section, dp = peer_of(step)
        pltpu.make_async_remote_copy(
            src_ref=send.at[section],
            dst_ref=slots.at[me],
            send_sem=send_sem,
            recv_sem=recv_sem,
            device_id={"section": section, "dp": dp},
        ).start()
        return unused

    lax.fori_loop(1, count, post, 0)
    pltpu.make_async_copy(send.at[my_section], slots.at[me], recv_sem).start()
    pltpu.make_async_copy(slots, slots, recv_sem).wait()

    wide[...] = slots[...].reshape(tokens * per_token, HD).astype(jnp.float32)
    for row in range(per_token):
        out_ref[row] = wide[pl.ds(row, tokens, stride=per_token), :].astype(out_ref.dtype)

    others = slots.at[pl.ds(0, count - 1)]
    pltpu.make_async_copy(others, others, send_sem).wait()


def attend_kernel(q_ref, kv_ref, seen_ref, gate_ref, out_ref):
    head = pl.program_id(0)
    heads = kv_ref.shape[0] // 2
    tokens = kv_ref.shape[1]
    rows = q_ref.shape[0]
    keys = kv_ref[head]
    vals = kv_ref[heads + head]
    seen = seen_ref[...]
    live = lax.broadcasted_iota(jnp.int32, (tokens, rows), 0) < seen
    gain = jnp.where(seen > 0, jnp.tanh(gate_ref[...]), 0.0)
    factor = LOG2E / math.sqrt(HD)
    for group in range(q_ref.shape[1] // HD):
        columns = slice(group * HD, (group + 1) * HD)
        scores = lax.dot_general(
            keys, q_ref[:, columns], (((1,), (1,)), ((), ())), preferred_element_type=jnp.float32
        )
        scores = jnp.where(live, scores * factor, -1e30)
        expo = jnp.exp2(scores - jnp.max(scores, axis=0, keepdims=True))
        denom = jnp.sum(expo, axis=0, keepdims=True)
        weights = (expo * (gain / denom)).astype(jnp.bfloat16)
        out_ref[:, columns] = lax.dot_general(
            weights, vals, (((0,), (0,)), ((), ())), preferred_element_type=jnp.float32
        ).astype(out_ref.dtype)


def body(queries, image_kv, visible, gate):
    sections = lax.axis_size("section")
    dps = lax.axis_size("dp")
    count = sections * dps
    img_dev, width = image_kv.shape[2:]
    heads = width // HD
    per_token = 2 * heads
    tokens = count * img_dev
    rows, columns = queries.shape[1:]
    block = columns // heads
    vmem = pl.BlockSpec(memory_space=pltpu.VMEM)
    gathered = pl.pallas_call(
        functools.partial(gather_kernel, sections, dps),
        out_shape=jax.ShapeDtypeStruct((per_token, tokens, HD), image_kv.dtype),
        in_specs=[vmem],
        out_specs=vmem,
        scratch_shapes=[
            pltpu.VMEM((sections, img_dev * per_token, HD), jnp.float32),
            pltpu.VMEM((sections, img_dev * per_token, HD), image_kv.dtype),
            pltpu.VMEM((count, img_dev * per_token, HD), image_kv.dtype),
            pltpu.VMEM((tokens * per_token, HD), jnp.float32),
            pltpu.SemaphoreType.DMA,
            pltpu.SemaphoreType.DMA,
        ],
        compiler_params=pltpu.CompilerParams(
            collective_id=0, has_side_effects=True, vmem_limit_bytes=40 * 1024 * 1024
        ),
        name="gather_kv",
    )(jnp.transpose(image_kv, (0, 2, 1, 3)))
    out = pl.pallas_call(
        attend_kernel,
        out_shape=jax.ShapeDtypeStruct((rows, columns), queries.dtype),
        grid=(heads,),
        in_specs=[
            pl.BlockSpec((rows, block), lambda k: (0, k)),
            pl.BlockSpec((per_token, tokens, HD), lambda k: (0, 0, 0)),
            pl.BlockSpec((1, rows), lambda k: (0, 0)),
            pl.BlockSpec((1, 1), lambda k: (0, 0)),
        ],
        out_specs=pl.BlockSpec((rows, block), lambda k: (0, k)),
        compiler_params=pltpu.CompilerParams(vmem_limit_bytes=40 * 1024 * 1024),
        name="attend",
    )(queries[0], gathered, visible.reshape(1, rows), gate.reshape(1, 1))
    return out[None]


def solution(mesh):
    in_specs = (
        P("section", "dp", None),
        P(None, None, ("section", "dp"), None),
        P("dp"),
        P("section"),
    )
    out_specs = P("section", "dp", None)
    return jax.shard_map(body, mesh=mesh, in_specs=in_specs, out_specs=out_specs, check_vma=False)
```

```python
import functools
import math

import jax
import jax.numpy as jnp
from jax import lax
from jax.experimental import pallas as pl
from jax.experimental.pallas import tpu as pltpu
from jax.sharding import PartitionSpec as P

HD = 128
LANES = 128
LOG2E = math.log2(math.e)


def gather_kernel(sections, dps, kv_ref, out_ref, stage, send, slots, wide, send_sem, recv_sem):
    count = sections * dps
    my_section = lax.axis_index("section")
    my_dp = lax.axis_index("dp")
    me = my_section * dps + my_dp
    img_dev = kv_ref.shape[1]
    heads = kv_ref.shape[3] // HD
    per_token = 2 * heads
    tokens = count * img_dev

    barrier = pltpu.get_barrier_semaphore()

    def peer_of(step):
        peer = lax.rem(me + step, count)
        return lax.div(peer, dps), lax.rem(peer, dps)

    def greet(step, unused):
        section, dp = peer_of(step)
        pl.semaphore_signal(barrier, inc=1, device_id={"section": section, "dp": dp})
        return unused

    lax.fori_loop(1, count, greet, 0)

    for layer in range(sections):
        for token in range(img_dev):
            rows = kv_ref[layer, token].astype(jnp.float32)
            for part in range(2):
                for head in range(heads):
                    at = token * per_token + part * heads + head
                    stage[layer, at : at + 1, :] = rows[part : part + 1, head * HD : (head + 1) * HD]
        send[layer] = stage[layer].astype(send.dtype)

    pl.semaphore_wait(barrier, count - 1)

    def post(step, unused):
        section, dp = peer_of(step)
        pltpu.make_async_remote_copy(
            src_ref=send.at[section],
            dst_ref=slots.at[me],
            send_sem=send_sem,
            recv_sem=recv_sem,
            device_id={"section": section, "dp": dp},
        ).start()
        return unused

    lax.fori_loop(1, count, post, 0)
    pltpu.make_async_copy(send.at[my_section], slots.at[me], recv_sem).start()
    pltpu.make_async_copy(slots, slots, recv_sem).wait()

    wide[...] = slots[...].reshape(tokens * per_token, HD).astype(jnp.float32)
    for row in range(per_token):
        out_ref[row] = wide[pl.ds(row, tokens, stride=per_token), :].astype(out_ref.dtype)

    others = slots.at[pl.ds(0, count - 1)]
    pltpu.make_async_copy(others, others, send_sem).wait()


def spread(block, pack):
    zeros = jnp.zeros_like(block)
    return jnp.concatenate(
        [
            jnp.concatenate([block if row == column else zeros for column in range(pack)], axis=1)
            for row in range(pack)
        ],
        axis=0,
    )


def attend_kernel(q_ref, kv_ref, seen_ref, gate_ref, out_ref):
    head = pl.program_id(0)
    heads = kv_ref.shape[0] // 2
    tokens = kv_ref.shape[1]
    rows = q_ref.shape[0]
    pack = math.gcd(q_ref.shape[1] // HD, max(1, LANES // tokens))
    width = pack * HD
    keys = spread(kv_ref[head], pack)
    vals = spread(kv_ref[heads + head], pack)
    seen = seen_ref[...]
    live = lax.broadcasted_iota(jnp.int32, (tokens, rows), 0) < seen
    gain = jnp.where(seen > 0, jnp.tanh(gate_ref[...]), 0.0)
    factor = LOG2E / math.sqrt(HD)
    spans = [slice(at, at + width) for at in range(0, q_ref.shape[1], width)]
    raw = [
        lax.dot_general(
            q_ref[:, span], keys, (((1,), (1,)), ((), ())), preferred_element_type=jnp.float32
        )
        for span in spans
    ]
    turned = [scores.T for scores in raw]
    weights = []
    for scores in turned:
        parts = []
        for at in range(0, pack * tokens, tokens):
            part = jnp.where(live, scores[at : at + tokens] * factor, -1e30)
            expo = jnp.exp2(part - jnp.max(part, axis=0, keepdims=True))
            denom = jnp.sum(expo, axis=0, keepdims=True)
            parts.append(expo * (gain / denom))
        weights.append(jnp.concatenate(parts, axis=0).T.astype(jnp.bfloat16))
    for span, part in zip(spans, weights):
        out_ref[:, span] = jnp.dot(part, vals, preferred_element_type=jnp.float32).astype(out_ref.dtype)


def body(queries, image_kv, visible, gate):
    sections = lax.axis_size("section")
    dps = lax.axis_size("dp")
    count = sections * dps
    img_dev, width = image_kv.shape[2:]
    heads = width // HD
    per_token = 2 * heads
    tokens = count * img_dev
    rows, columns = queries.shape[1:]
    block = columns // heads
    vmem = pl.BlockSpec(memory_space=pltpu.VMEM)
    gathered = pl.pallas_call(
        functools.partial(gather_kernel, sections, dps),
        out_shape=jax.ShapeDtypeStruct((per_token, tokens, HD), image_kv.dtype),
        in_specs=[vmem],
        out_specs=vmem,
        scratch_shapes=[
            pltpu.VMEM((sections, img_dev * per_token, HD), jnp.float32),
            pltpu.VMEM((sections, img_dev * per_token, HD), image_kv.dtype),
            pltpu.VMEM((count, img_dev * per_token, HD), image_kv.dtype),
            pltpu.VMEM((tokens * per_token, HD), jnp.float32),
            pltpu.SemaphoreType.DMA,
            pltpu.SemaphoreType.DMA,
        ],
        compiler_params=pltpu.CompilerParams(
            collective_id=0, has_side_effects=True, vmem_limit_bytes=32 * 1024 * 1024
        ),
        name="gather_kv",
    )(jnp.transpose(image_kv, (0, 2, 1, 3)))
    out = pl.pallas_call(
        attend_kernel,
        out_shape=jax.ShapeDtypeStruct((rows, columns), queries.dtype),
        grid=(heads,),
        in_specs=[
            pl.BlockSpec((rows, block), lambda k: (0, k)),
            pl.BlockSpec((per_token, tokens, HD), lambda k: (0, 0, 0)),
            pl.BlockSpec((1, rows), lambda k: (0, 0)),
            pl.BlockSpec((1, 1), lambda k: (0, 0)),
        ],
        out_specs=pl.BlockSpec((rows, block), lambda k: (0, k)),
        compiler_params=pltpu.CompilerParams(vmem_limit_bytes=60 * 1024 * 1024),
        name="attend",
    )(queries[0], gathered, visible.reshape(1, rows), gate.reshape(1, 1))
    return out[None]


def solution(mesh):
    in_specs = (
        P("section", "dp", None),
        P(None, None, ("section", "dp"), None),
        P("dp"),
        P("section"),
    )
    out_specs = P("section", "dp", None)
    return jax.shard_map(body, mesh=mesh, in_specs=in_specs, out_specs=out_specs, check_vma=False)
```

```python
import functools
import math

import jax
import jax.numpy as jnp
from jax import lax
from jax.experimental import pallas as pl
from jax.experimental.pallas import tpu as pltpu
from jax.sharding import PartitionSpec as P

HD = 128
LANES = 128
LOG2E = math.log2(math.e)


def gather_kernel(
    sections, dps, kv_ref, out_ref, held, stage, send, layer_kv, slots, wide, load_sem, send_sems, recv_sems
):
    my_section = lax.axis_index("section")
    my_dp = lax.axis_index("dp")
    img_dev = held.shape[1]
    heads = held.shape[3] // HD
    per_token = 2 * heads
    tokens = sections * dps * img_dev
    other_sections = [lax.rem(my_section + step, sections) for step in range(1, sections)]
    other_dps = [lax.rem(my_dp + step, dps) for step in range(1, dps)]

    load = pltpu.make_async_copy(kv_ref, held, load_sem)
    load.start()
    barrier = pltpu.get_barrier_semaphore()
    for dp in other_dps:
        pl.semaphore_signal(barrier, inc=1, device_id={"section": my_section, "dp": dp})
    for section in other_sections:
        pl.semaphore_signal(barrier, inc=1, device_id={"section": section, "dp": my_dp})
    load.wait()

    for layer in range(sections):
        for token in range(img_dev):
            rows = held[layer, token].astype(jnp.float32)
            for part in range(2):
                for head in range(heads):
                    at = token * per_token + part * heads + head
                    stage[layer, at : at + 1, :] = rows[part : part + 1, head * HD : (head + 1) * HD]
        send[layer] = stage[layer].astype(send.dtype)

    pl.semaphore_wait(barrier, sections + dps - 2)

    for section in other_sections:
        pltpu.make_async_remote_copy(
            src_ref=send.at[section],
            dst_ref=layer_kv.at[my_section],
            send_sem=send_sems.at[0],
            recv_sem=recv_sems.at[0],
            device_id={"section": section, "dp": my_dp},
        ).start()
    pltpu.make_async_copy(send.at[my_section], layer_kv.at[my_section], recv_sems.at[0]).start()
    pltpu.make_async_copy(layer_kv, layer_kv, recv_sems.at[0]).wait()

    mine = slots.at[:, my_dp]
    for dp in other_dps:
        pltpu.make_async_remote_copy(
            src_ref=layer_kv,
            dst_ref=mine,
            send_sem=send_sems.at[1],
            recv_sem=recv_sems.at[1],
            device_id={"section": my_section, "dp": dp},
        ).start()
    pltpu.make_async_copy(layer_kv, mine, recv_sems.at[1]).start()
    pltpu.make_async_copy(slots, slots, recv_sems.at[1]).wait()

    wide[...] = slots[...].reshape(tokens * per_token, HD).astype(jnp.float32)
    for row in range(per_token):
        out_ref[row] = wide[pl.ds(row, tokens, stride=per_token), :].astype(out_ref.dtype)

    sent = send.at[pl.ds(0, sections - 1)]
    pltpu.make_async_copy(sent, sent, send_sems.at[0]).wait()
    sent = slots.at[:, pl.ds(0, dps - 1)]
    pltpu.make_async_copy(sent, sent, send_sems.at[1]).wait()


def spread(block, pack):
    zeros = jnp.zeros_like(block)
    return jnp.concatenate(
        [
            jnp.concatenate([block if row == column else zeros for column in range(pack)], axis=1)
            for row in range(pack)
        ],
        axis=0,
    )


def attend_kernel(step_heads, q_ref, kv_ref, seen_ref, gate_ref, out_ref):
    heads = kv_ref.shape[0] // 2
    tokens = kv_ref.shape[1]
    rows, columns = q_ref.shape
    first = pl.program_id(0) * step_heads
    block = columns // step_heads
    pack = math.gcd(block // HD, max(1, LANES // tokens))
    width = pack * HD
    seen = seen_ref[...]
    live = lax.broadcasted_iota(jnp.int32, (tokens, rows), 0) < seen
    gain = jnp.where(seen > 0, jnp.tanh(gate_ref[...]), 0.0)
    factor = LOG2E / math.sqrt(HD)
    spans = [slice(at, at + width) for at in range(0, columns, width)]
    turned = []
    for head in range(step_heads):
        keys = spread(kv_ref[first + head], pack)
        for span in spans[head * (block // width) : (head + 1) * (block // width)]:
            scores = lax.dot_general(
                q_ref[:, span], keys, (((1,), (1,)), ((), ())), preferred_element_type=jnp.float32
            )
            turned.append(scores.T)
    weights = []
    for scores in turned:
        parts = []
        for at in range(0, pack * tokens, tokens):
            part = jnp.where(live, scores[at : at + tokens] * factor, -1e30)
            expo = jnp.exp2(part - jnp.max(part, axis=0, keepdims=True))
            denom = jnp.sum(expo, axis=0, keepdims=True)
            parts.append(expo * (gain / denom))
        weights.append(jnp.concatenate(parts, axis=0).T.astype(jnp.bfloat16))
    for head in range(step_heads):
        vals = spread(kv_ref[heads + first + head], pack)
        for at in range(head * (block // width), (head + 1) * (block // width)):
            out_ref[:, spans[at]] = jnp.dot(
                weights[at], vals, preferred_element_type=jnp.float32
            ).astype(out_ref.dtype)


def body(queries, image_kv, visible, gate):
    sections = lax.axis_size("section")
    dps = lax.axis_size("dp")
    count = sections * dps
    img_dev, width = image_kv.shape[2:]
    heads = width // HD
    per_token = 2 * heads
    tokens = count * img_dev
    rows, columns = queries.shape[1:]
    step_heads = math.gcd(heads, max(1, LANES // tokens))
    block = columns // heads * step_heads
    vmem = pl.BlockSpec(memory_space=pltpu.VMEM)
    gathered = pl.pallas_call(
        functools.partial(gather_kernel, sections, dps),
        out_shape=jax.ShapeDtypeStruct((per_token, tokens, HD), image_kv.dtype),
        in_specs=[pl.BlockSpec(memory_space=pl.ANY)],
        out_specs=vmem,
        scratch_shapes=[
            pltpu.VMEM((sections, img_dev, 2, width), image_kv.dtype),
            pltpu.VMEM((sections, img_dev * per_token, HD), jnp.float32),
            pltpu.VMEM((sections, img_dev * per_token, HD), image_kv.dtype),
            pltpu.VMEM((sections, img_dev * per_token, HD), image_kv.dtype),
            pltpu.VMEM((sections, dps, img_dev * per_token, HD), image_kv.dtype),
            pltpu.VMEM((tokens * per_token, HD), jnp.float32),
            pltpu.SemaphoreType.DMA,
            pltpu.SemaphoreType.DMA((2,)),
            pltpu.SemaphoreType.DMA((2,)),
        ],
        compiler_params=pltpu.CompilerParams(
            collective_id=0, has_side_effects=True, vmem_limit_bytes=60 * 1024 * 1024
        ),
        name="gather_kv",
    )(jnp.transpose(image_kv, (0, 2, 1, 3)))
    out = pl.pallas_call(
        functools.partial(attend_kernel, step_heads),
        out_shape=jax.ShapeDtypeStruct((rows, columns), queries.dtype),
        grid=(heads // step_heads,),
        in_specs=[
            pl.BlockSpec((rows, block), lambda k: (0, k)),
            pl.BlockSpec((per_token, tokens, HD), lambda k: (0, 0, 0)),
            pl.BlockSpec((1, rows), lambda k: (0, 0)),
            pl.BlockSpec((1, 1), lambda k: (0, 0)),
        ],
        out_specs=pl.BlockSpec((rows, block), lambda k: (0, k)),
        compiler_params=pltpu.CompilerParams(vmem_limit_bytes=60 * 1024 * 1024),
        name="attend",
    )(queries[0], gathered, visible.reshape(1, rows), gate.reshape(1, 1))
    return out[None]


def solution(mesh):
    in_specs = (
        P("section", "dp", None),
        P(None, None, ("section", "dp"), None),
        P("dp"),
        P("section"),
    )
    out_specs = P("section", "dp", None)
    return jax.shard_map(body, mesh=mesh, in_specs=in_specs, out_specs=out_specs, check_vma=False)
```

```python
import functools
import math

import jax
import jax.numpy as jnp
from jax import lax
from jax.experimental import pallas as pl
from jax.experimental.pallas import tpu as pltpu
from jax.sharding import PartitionSpec as P

HD = 128
LANES = 128
LOG2E = math.log2(math.e)


def gather_kernel(
    sections, dps, kv_ref, out_ref, held, stage, send, slots, wide, load_sem, send_sem, recv_sem
):
    my_section = lax.axis_index("section")
    my_dp = lax.axis_index("dp")
    img_dev = held.shape[1]
    heads = held.shape[3] // HD
    per_token = 2 * heads
    tokens = sections * dps * img_dev
    dp_ring = [lax.rem(my_dp + step, dps) for step in range(dps)]

    def for_peers(act):
        def one_section(step, unused):
            section = lax.rem(my_section + step, sections)
            for dp in dp_ring:
                act(section, dp)
            return unused

        lax.fori_loop(1, sections, one_section, 0)
        for dp in dp_ring[1:]:
            act(my_section, dp)

    load = pltpu.make_async_copy(kv_ref, held, load_sem)
    load.start()
    barrier = pltpu.get_barrier_semaphore()
    for_peers(
        lambda section, dp: pl.semaphore_signal(
            barrier, inc=1, device_id={"section": section, "dp": dp}
        )
    )
    load.wait()

    for layer in range(sections):
        for token in range(img_dev):
            rows = held[layer, token].astype(jnp.float32)
            for part in range(2):
                for head in range(heads):
                    at = token * per_token + part * heads + head
                    stage[layer, at : at + 1, :] = rows[part : part + 1, head * HD : (head + 1) * HD]
        send[layer] = stage[layer].astype(send.dtype)

    pl.semaphore_wait(barrier, sections * dps - 1)

    mine = slots.at[my_section * dps + my_dp]
    for_peers(
        lambda section, dp: pltpu.make_async_remote_copy(
            src_ref=send.at[section],
            dst_ref=mine,
            send_sem=send_sem,
            recv_sem=recv_sem,
            device_id={"section": section, "dp": dp},
        ).start()
    )
    pltpu.make_async_copy(send.at[my_section], mine, recv_sem).start()
    pltpu.make_async_copy(slots, slots, recv_sem).wait()

    wide[...] = slots[...].reshape(tokens * per_token, HD).astype(jnp.float32)
    for row in range(per_token):
        out_ref[row] = wide[pl.ds(row, tokens, stride=per_token), :].astype(out_ref.dtype)

    sent = slots.at[pl.ds(0, sections * dps - 1)]
    pltpu.make_async_copy(sent, sent, send_sem).wait()


def spread(block, pack):
    zeros = jnp.zeros_like(block)
    return jnp.concatenate(
        [
            jnp.concatenate([block if row == column else zeros for column in range(pack)], axis=1)
            for row in range(pack)
        ],
        axis=0,
    )


def attend_kernel(step_heads, q_ref, kv_ref, seen_ref, gate_ref, out_ref):
    heads = kv_ref.shape[0] // 2
    tokens = kv_ref.shape[1]
    rows, columns = q_ref.shape
    first = pl.program_id(0) * step_heads
    block = columns // step_heads
    pack = math.gcd(block // HD, max(1, LANES // tokens))
    width = pack * HD
    seen = seen_ref[...]
    live = lax.broadcasted_iota(jnp.int32, (tokens, rows), 0) < seen
    gain = jnp.where(seen > 0, jnp.tanh(gate_ref[...]), 0.0)
    factor = LOG2E / math.sqrt(HD)
    spans = [slice(at, at + width) for at in range(0, columns, width)]
    turned = []
    for head in range(step_heads):
        keys = spread(kv_ref[first + head], pack)
        for span in spans[head * (block // width) : (head + 1) * (block // width)]:
            scores = lax.dot_general(
                q_ref[:, span], keys, (((1,), (1,)), ((), ())), preferred_element_type=jnp.float32
            )
            turned.append(scores.T)
    weights = []
    for scores in turned:
        parts = []
        for at in range(0, pack * tokens, tokens):
            part = jnp.where(live, scores[at : at + tokens] * factor, -1e30)
            expo = jnp.exp2(part - jnp.max(part, axis=0, keepdims=True))
            denom = jnp.sum(expo, axis=0, keepdims=True)
            parts.append(expo * (gain / denom))
        weights.append(jnp.concatenate(parts, axis=0).T.astype(jnp.bfloat16))
    for head in range(step_heads):
        vals = spread(kv_ref[heads + first + head], pack)
        for at in range(head * (block // width), (head + 1) * (block // width)):
            out_ref[:, spans[at]] = jnp.dot(
                weights[at], vals, preferred_element_type=jnp.float32
            ).astype(out_ref.dtype)


def body(queries, image_kv, visible, gate):
    sections = lax.axis_size("section")
    dps = lax.axis_size("dp")
    count = sections * dps
    img_dev, width = image_kv.shape[2:]
    heads = width // HD
    per_token = 2 * heads
    tokens = count * img_dev
    rows, columns = queries.shape[1:]
    step_heads = math.gcd(heads, max(1, LANES // tokens))
    block = columns // heads * step_heads
    vmem = pl.BlockSpec(memory_space=pltpu.VMEM)
    gathered = pl.pallas_call(
        functools.partial(gather_kernel, sections, dps),
        out_shape=jax.ShapeDtypeStruct((per_token, tokens, HD), image_kv.dtype),
        in_specs=[pl.BlockSpec(memory_space=pl.ANY)],
        out_specs=vmem,
        scratch_shapes=[
            pltpu.VMEM((sections, img_dev, 2, width), image_kv.dtype),
            pltpu.VMEM((sections, img_dev * per_token, HD), jnp.float32),
            pltpu.VMEM((sections, img_dev * per_token, HD), image_kv.dtype),
            pltpu.VMEM((count, img_dev * per_token, HD), image_kv.dtype),
            pltpu.VMEM((tokens * per_token, HD), jnp.float32),
            pltpu.SemaphoreType.DMA,
            pltpu.SemaphoreType.DMA,
            pltpu.SemaphoreType.DMA,
        ],
        compiler_params=pltpu.CompilerParams(
            collective_id=0, has_side_effects=True, vmem_limit_bytes=60 * 1024 * 1024
        ),
        name="gather_kv",
    )(jnp.transpose(image_kv, (0, 2, 1, 3)))
    out = pl.pallas_call(
        functools.partial(attend_kernel, step_heads),
        out_shape=jax.ShapeDtypeStruct((rows, columns), queries.dtype),
        grid=(heads // step_heads,),
        in_specs=[
            pl.BlockSpec((rows, block), lambda k: (0, k)),
            pl.BlockSpec((per_token, tokens, HD), lambda k: (0, 0, 0)),
            pl.BlockSpec((1, rows), lambda k: (0, 0)),
            pl.BlockSpec((1, 1), lambda k: (0, 0)),
        ],
        out_specs=pl.BlockSpec((rows, block), lambda k: (0, k)),
        compiler_params=pltpu.CompilerParams(vmem_limit_bytes=60 * 1024 * 1024),
        name="attend",
    )(queries[0], gathered, visible.reshape(1, rows), gate.reshape(1, 1))
    return out[None]


def solution(mesh):
    in_specs = (
        P("section", "dp", None),
        P(None, None, ("section", "dp"), None),
        P("dp"),
        P("section"),
    )
    out_specs = P("section", "dp", None)
    return jax.shard_map(body, mesh=mesh, in_specs=in_specs, out_specs=out_specs, check_vma=False)
```
